32 devices in a mesh: ia: 4 (over z), ja: 4 (over x, core), ka: 2 (over y).
Axes of the slice: x: 2, y: 2, z: 4, core: 2. Of those that a mesh axis runs over, the one named last changes fastest.
Arguments:
- tensor: float32 [512, 256, 512], P('ia', 'ja', 'ka'), may hold values from -6 to 6
- factor_b: float32 [4, 64, 256], P('ja', ('ia', 'ka')), may hold values from -0.375 to 0.375
- factor_c: float32 [2, 256, 256], P('ka', ('ia', 'ja')), may hold values from -0.25 to 0.25
Outputs:
- new_a: float32 [4, 128, 256], P('ia', ('ja', 'ka'))
- new_b: float32 [4, 64, 256], P('ja', ('ia', 'ka'))
- new_c: float32 [2, 256, 256], P('ka', ('ia', 'ja'))
The draws below stay inside these ranges and needn't reach their ends.
All inputs are finite; a program needn't handle non-finite values.
Results may differ from the reference program's by a relative error of at most 0.00011.
Values sent between devices are 32-bit elements; how exact they have to be, the bound alone decides.
No kernel may reach another device: no remote copies, remote signals or barrier semaphores. Data moves between devices by JAX's collectives and lax.ppermute only.
A program may use at most 64 MiB of HBM per device.

```python
import jax
import jax.numpy as jnp
from jax import lax

I_DEV = 128
J_DEV = 64
K_DEV = 256
R = 256
I = 512
J = 256
K = 512
N_IA = 4
N_JA = 4
N_KA = 2


def level_of(own_key, extent, pieces, smallest, high):
    level, own = 1.0, jax.random.fold_in(own_key, 6)
    for axis_at, shards_of in pieces:
        heights = jnp.exp(jax.random.uniform(jax.random.fold_in(own, axis_at), (shards_of,), jnp.float32, smallest / len(pieces), high / len(pieces)))
        level = level * jnp.repeat(heights, extent[axis_at] // shards_of).reshape([-1 if axis == axis_at else 1 for axis in range(len(extent))])
    return level


def centred(rng, shape, width, limit, cuts=(), dtype=jnp.bfloat16):
    array = jax.random.normal(rng, shape, jnp.float32) * width
    if len(cuts) > 0:
        array = level_of(rng, shape, cuts, -0.22, 0.18) * array
    return jnp.clip(array, min=-limit, max=limit).astype(dtype)


def setup_inputs(seed: int = 0) -> dict:
    keys = jax.random.split(jax.random.key(seed), 4)
    tensor = centred(keys[0], (I, J, K), 1.0, 6.0, ((0, 4), (1, 4), (2, 2)), jnp.float32)
    factor_b = centred(keys[1], (N_JA, J_DEV, R), J ** -0.5, 0.375, ((0, 4), (1, 8)), jnp.float32)
    factor_c = centred(keys[2], (N_KA, K_DEV, R), K ** -0.5, 0.25, ((0, 2), (1, 16)), jnp.float32)
    return {"tensor": tensor, "factor_b": factor_b, "factor_c": factor_c}


HIGH = lax.Precision.HIGHEST

def gram_of(rows):
    return jnp.dot(rows.T.astype(jnp.float32), rows.astype(jnp.float32), precision=HIGH, preferred_element_type=jnp.float32)

def solve_rows(right, gram):
    factor = jnp.linalg.cholesky(gram)
    return jax.scipy.linalg.cho_solve((factor, True), right.T).T

def reference(tensor, factor_b, factor_c):
    mat_b = factor_b.reshape(J, R)
    mat_c = factor_c.reshape(K, R)
    gram_b = gram_of(mat_b)
    gram_c = gram_of(mat_c)
    blocks = tensor.reshape(N_IA, I_DEV, J, K)

    def first(block):
        inner = jnp.einsum('ijk,kr->ijr', block, mat_c, precision=HIGH)
        return jnp.einsum('ijr,jr->ir', inner, mat_b, precision=HIGH)
    mttkrp_a = lax.map(first, blocks).reshape(I, R)
    mat_a = solve_rows(mttkrp_a, gram_b * gram_c)
    gram_a = gram_of(mat_a)
    rows_a = mat_a.reshape(N_IA, I_DEV, R)

    def second(total, pair):
        block, part_a = pair
        inner = jnp.einsum('ijk,kr->ijr', block, mat_c, precision=HIGH)
        return (total + jnp.einsum('ijr,ir->jr', inner, part_a, precision=HIGH), None)
    mttkrp_b, unused = lax.scan(second, jnp.zeros((J, R), jnp.float32), (blocks, rows_a))
    mat_b2 = solve_rows(mttkrp_b, gram_a * gram_c)
    gram_b2 = gram_of(mat_b2)

    def third(total, pair):
        block, part_a = pair
        weights = part_a[:, None, :] * mat_b2[None, :, :]
        return (total + jnp.einsum('ijk,ijr->kr', block, weights, precision=HIGH), None)
    mttkrp_c, unused = lax.scan(third, jnp.zeros((K, R), jnp.float32), (blocks, rows_a))
    mat_c2 = solve_rows(mttkrp_c, gram_a * gram_b2)
    return (mat_a.reshape(N_IA, I_DEV, R), mat_b2.reshape(N_JA, J_DEV, R), mat_c2.reshape(N_KA, K_DEV, R))
```

```python
import functools

import jax
import jax.numpy as jnp
from jax import lax
from jax.experimental import pallas as pl
from jax.experimental.pallas import tpu as pltpu
from jax.sharding import PartitionSpec as P

HIGH = lax.Precision.HIGHEST
F32 = jnp.float32
BF16 = jnp.bfloat16
VMEM_LIMIT = 28 * 1024 * 1024
NN = (((1,), (0,)), ((), ()))
NT = (((1,), (1,)), ((), ()))
TN = (((0,), (0,)), ((), ()))


def mul(left, right, dims=NN):
    return lax.dot_general(left, right, dims, precision=HIGH, preferred_element_type=F32)


def split(value):
    high = value.astype(BF16)
    return high, (value - high.astype(F32)).astype(BF16)


def tree(values):
    values = list(values)
    while len(values) > 1:
        values = [a + b for a, b in zip(values[::2], values[1::2])]
    return values[0]


def bits(axis, count):
    assert count & (count - 1) == 0
    return [(axis, 1 << at) for at in reversed(range(count.bit_length() - 1))]


def swap(value, axis, distance):
    return lax.ppermute(value, axis, [(rank, rank ^ distance) for rank in range(lax.axis_size(axis))])


def grow(block, stages):
    for axis, distance in stages:
        block = jnp.concatenate([block, swap(block, axis, distance)], axis=0)
    return block


def origin(place, stages):
    masks = {}
    for at, (axis, distance) in enumerate(stages):
        masks[axis] = masks.get(axis, 0) ^ (distance if place >> at & 1 else 0)
    return masks


def invert_half(ref, which):
    size = 128
    count = size // 8
    lane = lax.broadcasted_iota(jnp.int32, (8, size), 1)
    sub = lax.broadcasted_iota(jnp.int32, (8, size), 0)
    rows = [ref[which, 8 * at : 8 * at + 8, :] for at in range(count)]

    def over_lanes(value, at):
        return jnp.broadcast_to(value[:, at : at + 1], (8, size))

    def over_rows(value, at):
        return jnp.broadcast_to(value[at : at + 1, :], (8, size))

    for t in range(count):
        row = rows[t]
        cols = [over_lanes(row, 8 * t + j) for j in range(8)]
        for k in range(8):
            pivot = 1.0 / over_rows(cols[k], k)
            here = sub == k
            row = jnp.where(lane == 8 * t + k, jnp.where(here, 1.0, 0.0), row)
            scaled = over_rows(row, k) * pivot
            row = jnp.where(here, scaled, row - cols[k] * scaled)
            for j in range(k + 1, 8):
                entry = over_rows(cols[j], k) * pivot
                cols[j] = jnp.where(here, entry, cols[j] - cols[k] * entry)
        rows[t] = row
        spread = [over_rows(row, j) for j in range(8)]
        inside = (lane >= 8 * t) & (lane < 8 * t + 8)
        for i in range(count):
            if i != t:
                terms = [over_lanes(rows[i], 8 * t + j) * spread[j] for j in range(8)]
                rows[i] = jnp.where(inside, 0.0, rows[i]) - tree(terms)
    for at in range(count):
        ref[which, 8 * at : 8 * at + 8, :] = rows[at]


def invert_first(m_ref, half_ref, cross_ref):
    h = m_ref.shape[0] // 2
    half_ref[0] = m_ref[:h, :h]
    invert_half(half_ref, 0)
    cross = mul(half_ref[0], m_ref[:h, h:])
    cross_ref[...] = cross
    half_ref[1] = m_ref[h:, h:] - mul(m_ref[h:, :h], cross)


def invert_last(half_ref, cross_ref, out_ref):
    h = cross_ref.shape[0]
    invert_half(half_ref, 1)
    cross, last = cross_ref[...], half_ref[1]
    corner = mul(cross, last)
    out_ref[:h, :h] = half_ref[0] + mul(corner, cross, NT)
    out_ref[:h, h:] = -corner
    out_ref[h:, :h] = -mul(last, cross, NT)
    out_ref[h:, h:] = last


def invert_scratch(rank):
    h = rank // 2
    return [pltpu.VMEM((rank, rank), F32), pltpu.VMEM((2, h, h), F32), pltpu.VMEM((h, h), F32)]


def on_device(n_ia, n_ja, n_ka, tensor, factor_b, factor_c):
    i_dev, j_dev, k_dev = tensor.shape
    rank = factor_b.shape[-1]
    n_a, n_b, n_c = n_ja * n_ka, n_ia * n_ka, n_ia * n_ja
    a_rows, b_rows, c_rows = i_dev // n_a, j_dev // n_b, k_dev // n_c
    h = rank // 2
    packed = h + h // 2
    ia_bits, ja_bits, ka_bits = bits("ia", n_ia), bits("ja", n_ja), bits("ka", n_ka)
    place = jnp.stack([lax.axis_index(axis) for axis in ("ia", "ja", "ka")]).astype(jnp.int32)
    vmem = pl.BlockSpec(memory_space=pltpu.VMEM)
    smem = pl.BlockSpec(memory_space=pltpu.SMEM)
    i_step = 16
    steps = i_dev // i_step
    depth = i_step * j_dev
    size = i_dev * j_dev * k_dev

    def span(s, length):
        return pl.ds(pl.multiple_of(s * length, length), length)

    def call(kernel, name, ins, outs, grid=(), in_specs=None, out_specs=None, scratch=(), flops=0, moved=1 << 20):
        in_specs = in_specs or [vmem] * len(ins)
        out_specs = out_specs or [vmem] * len(outs)
        return pl.pallas_call(
            kernel,
            grid=grid,
            out_shape=[jax.ShapeDtypeStruct(shape, dtype) for shape, dtype in outs],
            in_specs=in_specs,
            out_specs=out_specs,
            scratch_shapes=list(scratch),
            compiler_params=pltpu.CompilerParams(vmem_limit_bytes=VMEM_LIMIT),
            cost_estimate=pl.CostEstimate(flops=flops, bytes_accessed=moved, transcendentals=0),
            name=name,
        )(*ins)

    def pack_kernel(c_ref, b_ref, out_ref, c_buffer, b_buffer, sems):
        copies = [
            pltpu.make_async_copy(c_ref, c_buffer, sems.at[0]),
            pltpu.make_async_copy(b_ref, b_buffer, sems.at[1]),
        ]
        for copy in copies:
            copy.start()
        for copy in copies:
            copy.wait()
        out_ref[:c_rows, :] = c_buffer[0]
        out_ref[c_rows:, :] = b_buffer[0]

    hbm = pl.BlockSpec(memory_space=pltpu.HBM)
    (given,) = call(
        pack_kernel,
        "pack",
        [pltpu.with_memory_space_constraint(factor, pltpu.HBM) for factor in (factor_c, factor_b)],
        [((c_rows + b_rows, rank), F32)],
        in_specs=[hbm, hbm],
        scratch=[pltpu.VMEM(factor_c.shape, F32), pltpu.VMEM(factor_b.shape, F32), pltpu.SemaphoreType.DMA((2,))],
    )
    others = [swap(given, "ia", q) for q in range(1, n_ia)]

    def load_kernel(t_ref, high_ref, low_ref, buffer_ref, sems):
        copies = [
            pltpu.make_async_copy(
                t_ref.at[pl.ds(s * i_step, i_step)], buffer_ref.at[pl.ds(s * i_step, i_step)], sems.at[s]
            )
            for s in range(steps)
        ]
        for copy in copies:
            copy.start()
        for s, copy in enumerate(copies):
            copy.wait()
            high, low = split(buffer_ref[s * i_step : (s + 1) * i_step].reshape(depth, k_dev))
            high_ref[s * depth : (s + 1) * depth, :] = high
            low_ref[s * depth : (s + 1) * depth, :] = low

    t_parts = call(
        load_kernel,
        "load",
        [pltpu.with_memory_space_constraint(tensor, pltpu.HBM)],
        [((i_dev * j_dev, k_dev), BF16)] * 2,
        in_specs=[hbm],
        scratch=[pltpu.VMEM((i_dev, j_dev, k_dev), F32), pltpu.SemaphoreType.DMA((steps,))],
        moved=8 * size,
    )
    *others, t_high, t_low = lax.optimization_barrier((*others, *t_parts))
    both = jnp.stack([given, *others])
    c_blocks = grow(both[:, :c_rows].reshape(n_ia * c_rows, rank), ja_bits)
    b_blocks = grow(both[:, c_rows:].reshape(n_ia * b_rows, rank), ka_bits)

    def given_kernel(place_ref, c_ref, b_ref, gram_ref, tall_ref, b_out, whole_c, whole_b):
        left, right = c_ref[:, :h], c_ref[:, h:]
        gram_ref[:h, :] = mul(left, left, TN)
        gram_ref[h : 2 * h, :] = mul(left, right, TN)
        gram_ref[2 * h :, :] = mul(right, right, TN)
        ia, ja, ka = place_ref[0], place_ref[1], place_ref[2]
        for p in range(n_c):
            masks = origin(p, ia_bits[::-1] + ja_bits)
            whole_c[(ia ^ masks["ia"]) * n_ja + (ja ^ masks["ja"])] = c_ref[p * c_rows : (p + 1) * c_rows, :]
        for p in range(n_b):
            masks = origin(p, ia_bits[::-1] + ka_bits)
            whole_b[(ia ^ masks["ia"]) * n_ka + (ka ^ masks["ka"])] = b_ref[p * b_rows : (p + 1) * b_rows, :]
        b_out[...] = whole_b[...].reshape(j_dev, rank)
        high, low = split(whole_c[...].reshape(k_dev, rank))
        tall_ref[:k_dev, :] = high
        tall_ref[k_dev : 2 * k_dev, :] = high
        tall_ref[2 * k_dev :, :] = low

    gram_c_part, tall, b_slice = call(
        given_kernel,
        "given",
        [place, c_blocks, b_blocks],
        [((3 * h, h), F32), ((3 * k_dev, rank), BF16), ((j_dev, rank), F32)],
        in_specs=[smem, vmem, vmem],
        scratch=[pltpu.VMEM((n_c, c_rows, rank), F32), pltpu.VMEM((n_b, b_rows, rank), F32)],
        flops=2 * 6 * k_dev * rank * rank,
    )
    gram_c = gram_c_part
    for axis, distance in ka_bits:
        gram_c = gram_c + swap(gram_c, axis, distance)
    all_b = grow(b_blocks, ja_bits[::-1])

    def first_kernel(high_ref, low_ref, tall_ref, b_ref, y_ref, out_ref):
        def step(s, _):
            high, low = high_ref[span(s, depth), :], low_ref[span(s, depth), :]
            wide = jnp.concatenate([high, low, high], axis=1)
            inner = lax.dot_general(wide, tall_ref[...], NN, preferred_element_type=F32).reshape(i_step, j_dev, rank)
            y_ref[span(s, i_step)] = inner
            out_ref[span(s, i_step), :] = jnp.sum(inner * b_ref[...].reshape(1, j_dev, rank), axis=1)
            return 0

        lax.fori_loop(0, steps, step, 0)

    y, parts_a = call(
        first_kernel,
        "first",
        [t_high, t_low, tall, b_slice],
        [((i_dev, j_dev, rank), F32), ((i_dev, rank), F32)],
        flops=6 * size * rank,
        moved=8 * size,
    )

    def invert_a_first_kernel(packed_ref, b_ref, half_ref, cross_ref, gram_ref, m_ref):
        gram_ref[:h, :h] = packed_ref[:h, :]
        gram_ref[:h, h:] = packed_ref[h : 2 * h, :]
        gram_ref[h:, :h] = packed_ref[h : 2 * h, :].T
        gram_ref[h:, h:] = packed_ref[2 * h :, :]
        b = b_ref[...]
        m_ref[...] = gram_ref[...] * mul(b, b, TN)
        invert_first(m_ref, half_ref, cross_ref)

    halves, cross, gram_c = call(
        invert_a_first_kernel,
        "invert_a_first",
        [gram_c, all_b],
        [((2, h, h), F32), ((h, h), F32), ((rank, rank), F32)],
        scratch=[pltpu.VMEM((rank, rank), F32)],
        flops=5 * 1000 * 1000 * 1000,
    )

    def invert_last_kernel(half_in, cross_ref, out_ref, half_ref):
        half_ref[...] = half_in[...]
        invert_last(half_ref, cross_ref, out_ref)

    stages = [pair for pair in ja_bits if pair[1] > 1] + ka_bits + [pair for pair in ja_bits if pair[1] == 1]
    for at, (axis, distance) in enumerate(stages[:-1]):
        other_a = swap(parts_a, axis, distance)
        if at == 0:
            halves, cross, other_a = lax.optimization_barrier((halves, cross, other_a))
            (inverse_a,) = call(
                invert_last_kernel,
                "invert_a_last",
                [halves, cross],
                [((rank, rank), F32)],
                scratch=[pltpu.VMEM((2, h, h), F32)],
                flops=5 * 1000 * 1000 * 1000,
            )
        if at == 1:
            inverse_a, other_a = lax.optimization_barrier((inverse_a, other_a))
        parts_a = parts_a + other_a
    other_a = swap(parts_a, *stages[-1])

    def solve_a_kernel(place_ref, one_ref, other_ref, inverse_ref, a_ref, own_ref, gram_ref, rows_ref, packed_ref):
        a = mul(one_ref[...] + other_ref[...], inverse_ref[...])
        a_ref[...] = a
        rows_ref[...] = a.reshape(n_a, a_rows, rank)
        own_ref[...] = rows_ref[place_ref[1] * n_ka + place_ref[2]]
        left, right = a[:, :h], a[:, h:]
        middle = mul(left, right, TN)
        packed_ref[0, :h, :] = mul(left, left, TN)
        packed_ref[0, h:, :] = middle[: h // 2]
        packed_ref[1, :h, :] = mul(right, right, TN)
        packed_ref[1, h:, :] = middle[h // 2 :]
        gram_ref[...] = packed_ref[place_ref[1] & 1]

    a_slice, new_a, gram_a = call(
        solve_a_kernel,
        "solve_a",
        [place, parts_a, other_a, inverse_a],
        [((i_dev, rank), F32), ((a_rows, rank), F32), ((packed, h), F32)],
        in_specs=[smem, vmem, vmem, vmem],
        scratch=[pltpu.VMEM((n_a, a_rows, rank), F32), pltpu.VMEM((2, packed, h), F32)],
    )
    far_gram = swap(gram_a, *ia_bits[0])

    def second_kernel(y_ref, a_ref, out_ref):
        def step(s, total):
            return total + jnp.sum(y_ref[span(s, i_step)] * a_ref[span(s, i_step), :][:, None, :], axis=0)

        out_ref[...] = lax.fori_loop(0, steps, step, jnp.zeros((j_dev, rank), F32))

    (parts_b,) = call(
        second_kernel,
        "second",
        [y, a_slice],
        [((j_dev, rank), F32)],
        flops=2 * i_dev * j_dev * rank,
        moved=4 * i_dev * j_dev * rank,
    )
    t_high, t_low, parts_b = lax.optimization_barrier((t_high, t_low, parts_b))

    def turn_kernel(high_ref, low_ref, out_ref):
        def step(s, _):
            out_ref[:k_dev, span(s, depth)] = high_ref[span(s, depth), :].T
            out_ref[k_dev:, span(s, depth)] = low_ref[span(s, depth), :].T
            return 0

        lax.fori_loop(0, steps, step, 0)

    (turned,) = call(
        turn_kernel, "turn", [t_high, t_low], [((2 * k_dev, i_dev * j_dev), BF16)], moved=8 * size
    )
    stages_b = ka_bits + ia_bits
    other_b = swap(parts_b, *stages_b[0])
    far_gram, turned, other_b = lax.optimization_barrier((far_gram, turned, other_b))
    gram_a = gram_a + far_gram
    parts_b = parts_b + other_b
    for axis, distance in ia_bits[1:]:
        near_gram = swap(gram_a, axis, distance)
        gram_a = gram_a + near_gram
    gram_a_other = swap(gram_a, "ja", 1)

    def invert_b_first_kernel(place_ref, one_ref, other_ref, gram_c_ref, gram_ref, half_ref, cross_ref, packed_ref, m_ref):
        core = place_ref[1] & 1
        packed_ref[core] = one_ref[...]
        packed_ref[core ^ 1] = other_ref[...]
        gram_ref[:h, :h] = packed_ref[0, :h, :]
        gram_ref[h:, h:] = packed_ref[1, :h, :]
        gram_ref[: h // 2, h:] = packed_ref[0, h:, :]
        gram_ref[h // 2 : h, h:] = packed_ref[1, h:, :]
        gram_ref[h:, :h] = gram_ref[:h, h:].T
        m_ref[...] = gram_ref[...] * gram_c_ref[...]
        invert_first(m_ref, half_ref, cross_ref)

    gram_a, halves, cross = call(
        invert_b_first_kernel,
        "invert_b_first",
        [place, gram_a, gram_a_other, gram_c],
        [((rank, rank), F32), ((2, h, h), F32), ((h, h), F32)],
        in_specs=[smem, vmem, vmem, vmem],
        scratch=[pltpu.VMEM((2, packed, h), F32), pltpu.VMEM((rank, rank), F32)],
        flops=5 * 1000 * 1000 * 1000,
    )

    for at, (axis, distance) in enumerate(stages_b[1:-1], 1):
        other_b = swap(parts_b, axis, distance)
        if at == len(stages_b) - 2:
            halves, cross, other_b = lax.optimization_barrier((halves, cross, other_b))
        parts_b = parts_b + other_b
    other_b = swap(parts_b, *stages_b[-1])
    (inverse_b,) = call(
        invert_last_kernel,
        "invert_b_last",
        [halves, cross],
        [((rank, rank), F32)],
        scratch=[pltpu.VMEM((2, h, h), F32)],
        flops=5 * 1000 * 1000 * 1000,
    )

    def solve_b_kernel(place_ref, one_ref, other_ref, inverse_ref, b_ref, own_ref, rows_ref):
        b = mul(one_ref[...] + other_ref[...], inverse_ref[...])
        b_ref[...] = b
        rows_ref[...] = b.reshape(n_b, b_rows, rank)
        own_ref[...] = rows_ref[place_ref[0] * n_ka + place_ref[2]]

    b_new_slice, new_b = call(
        solve_b_kernel,
        "solve_b",
        [place, parts_b, other_b, inverse_b],
        [((j_dev, rank), F32), ((b_rows, rank), F32)],
        in_specs=[smem, vmem, vmem, vmem],
        scratch=[pltpu.VMEM((n_b, b_rows, rank), F32)],
    )

    first_b = swap(b_new_slice, *ja_bits[0])

    def third_kernel(turned_ref, a_ref, b_ref, out_ref):
        def step(s, total):
            high, low = split((a_ref[span(s, i_step), :][:, None, :] * b_ref[...][None]).reshape(depth, rank))
            both = lax.dot_general(turned_ref[:, span(s, depth)], high, NN, preferred_element_type=F32)
            more = lax.dot_general(turned_ref[:k_dev, span(s, depth)], low, NN, preferred_element_type=F32)
            return total + (both[:k_dev] + (both[k_dev:] + more))

        out_ref[...] = lax.fori_loop(0, steps, step, jnp.zeros((k_dev, rank), F32))

    (parts_c,) = call(
        third_kernel,
        "third",
        [turned, a_slice, b_new_slice],
        [((k_dev, rank), F32)],
        flops=6 * size * rank,
        moved=4 * size,
    )
    first_b, parts_c = lax.optimization_barrier((first_b, parts_c))
    all_b_new = grow(jnp.concatenate([b_new_slice, first_b], axis=0), ja_bits[1:])
    sums_c = lax.all_to_all(parts_c.reshape(n_c, c_rows, rank), ("ia", "ja"), split_axis=0, concat_axis=0)

    def invert_c_kernel(b_ref, gram_a_ref, inverse_ref, m_ref, half_ref, cross_ref):
        b = b_ref[...]
        m_ref[...] = gram_a_ref[...] * mul(b, b, TN)
        invert_first(m_ref, half_ref, cross_ref)
        invert_last(half_ref, cross_ref, inverse_ref)

    (inverse_c,) = call(
        invert_c_kernel,
        "invert_c",
        [all_b_new, gram_a],
        [((rank, rank), F32)],
        scratch=invert_scratch(rank),
        flops=10 * 1000 * 1000 * 1000,
    )

    def solve_c_kernel(sums_ref, inverse_ref, out_ref):
        out_ref[...] = mul(tree(sums_ref[q] for q in range(n_c)), inverse_ref[...])

    (new_c,) = call(solve_c_kernel, "solve_c", [sums_c, inverse_c], [((c_rows, rank), F32)])
    return (new_a[None], new_b[None], new_c[None])


def solution(mesh):
    sizes = [mesh.shape[axis] for axis in ("ia", "ja", "ka")]
    return jax.shard_map(
        functools.partial(on_device, *sizes),
        mesh=mesh,
        in_specs=(P("ia", "ja", "ka"), P("ja", ("ia", "ka"), None), P("ka", ("ia", "ja"), None)),
        out_specs=(
            P("ia", ("ja", "ka"), None),
            P("ja", ("ia", "ka"), None),
            P("ka", ("ia", "ja"), None),
        ),
        check_vma=False,
    )
```

```python
import functools

import jax
import jax.numpy as jnp
from jax import lax
from jax.experimental import pallas as pl
from jax.experimental.pallas import tpu as pltpu
from jax.sharding import PartitionSpec as P

HIGH = lax.Precision.HIGHEST
F32 = jnp.float32
BF16 = jnp.bfloat16
VMEM_LIMIT = 28 * 1024 * 1024
NN = (((1,), (0,)), ((), ()))
NT = (((1,), (1,)), ((), ()))
TN = (((0,), (0,)), ((), ()))


def mul(left, right, dims=NN):
    return lax.dot_general(left, right, dims, precision=HIGH, preferred_element_type=F32)


def split(value):
    high = value.astype(BF16)
    return high, (value - high.astype(F32)).astype(BF16)


def mul3(left, right, dims=NN):
    (left_high, left_low), (right_high, right_low) = split(left), split(right)
    left = jnp.concatenate([left_high, left_low, left_high], axis=dims[0][0][0])
    right = jnp.concatenate([right_high, right_high, right_low], axis=dims[0][1][0])
    return lax.dot_general(left, right, dims, preferred_element_type=F32)


def tree(values):
    values = list(values)
    while len(values) > 1:
        values = [a + b for a, b in zip(values[::2], values[1::2])]
    return values[0]


def bits(axis, count):
    assert count & (count - 1) == 0
    return [(axis, 1 << at) for at in reversed(range(count.bit_length() - 1))]


def swap(value, axis, distance):
    return lax.ppermute(value, axis, [(rank, rank ^ distance) for rank in range(lax.axis_size(axis))])


def grow(block, stages):
    for axis, distance in stages:
        block = jnp.concatenate([block, swap(block, axis, distance)], axis=0)
    return block


def origin(place, stages):
    masks = {}
    for at, (axis, distance) in enumerate(stages):
        masks[axis] = masks.get(axis, 0) ^ (distance if place >> at & 1 else 0)
    return masks


def invert_half(ref, which):
    size = 128
    count = size // 8
    lane = lax.broadcasted_iota(jnp.int32, (8, size), 1)
    sub = lax.broadcasted_iota(jnp.int32, (8, size), 0)
    rows = [ref[which, 8 * at : 8 * at + 8, :] for at in range(count)]

    def over_lanes(value, at):
        return jnp.broadcast_to(value[:, at : at + 1], (8, size))

    def over_rows(value, at):
        return jnp.broadcast_to(value[at : at + 1, :], (8, size))

    for t in range(count):
        row = rows[t]
        cols = [over_lanes(row, 8 * t + j) for j in range(8)]
        for k in range(8):
            pivot = 1.0 / over_rows(cols[k], k)
            here = sub == k
            row = jnp.where(lane == 8 * t + k, jnp.where(here, 1.0, 0.0), row)
            scaled = over_rows(row, k) * pivot
            row = jnp.where(here, scaled, row - cols[k] * scaled)
            for j in range(k + 1, 8):
                entry = over_rows(cols[j], k) * pivot
                cols[j] = jnp.where(here, entry, cols[j] - cols[k] * entry)
        rows[t] = row
        spread = [over_rows(row, j) for j in range(8)]
        inside = (lane >= 8 * t) & (lane < 8 * t + 8)
        for i in range(count):
            if i != t:
                terms = [over_lanes(rows[i], 8 * t + j) * spread[j] for j in range(8)]
                rows[i] = jnp.where(inside, 0.0, rows[i]) - tree(terms)
    for at in range(count):
        ref[which, 8 * at : 8 * at + 8, :] = rows[at]


def invert_first(m_ref, half_ref, cross_ref):
    h = m_ref.shape[0] // 2
    half_ref[0] = m_ref[:h, :h]
    invert_half(half_ref, 0)
    cross = mul(half_ref[0], m_ref[:h, h:])
    cross_ref[...] = cross
    half_ref[1] = m_ref[h:, h:] - mul(m_ref[h:, :h], cross)


def invert_last(half_ref, cross_ref, out_ref):
    h = cross_ref.shape[0]
    invert_half(half_ref, 1)
    cross, last = cross_ref[...], half_ref[1]
    corner = mul(cross, last)
    out_ref[:h, :h] = half_ref[0] + mul(corner, cross, NT)
    out_ref[:h, h:] = -corner
    out_ref[h:, :h] = -mul(last, cross, NT)
    out_ref[h:, h:] = last


def invert_scratch(rank):
    h = rank // 2
    return [pltpu.VMEM((rank, rank), F32), pltpu.VMEM((2, h, h), F32), pltpu.VMEM((h, h), F32)]


def on_device(n_ia, n_ja, n_ka, tensor, factor_b, factor_c):
    i_dev, j_dev, k_dev = tensor.shape
    rank = factor_b.shape[-1]
    n_a, n_b, n_c = n_ja * n_ka, n_ia * n_ka, n_ia * n_ja
    a_rows, b_rows, c_rows = i_dev // n_a, j_dev // n_b, k_dev // n_c
    h = rank // 2
    packed = h + h // 2
    ia_bits, ja_bits, ka_bits = bits("ia", n_ia), bits("ja", n_ja), bits("ka", n_ka)
    place = jnp.stack([lax.axis_index(axis) for axis in ("ia", "ja", "ka")]).astype(jnp.int32)
    vmem = pl.BlockSpec(memory_space=pltpu.VMEM)
    smem = pl.BlockSpec(memory_space=pltpu.SMEM)
    i_step = 16
    steps = i_dev // i_step
    depth = i_step * j_dev
    size = i_dev * j_dev * k_dev

    def span(s, length):
        return pl.ds(pl.multiple_of(s * length, length), length)

    def call(kernel, name, ins, outs, grid=(), in_specs=None, out_specs=None, scratch=(), flops=0, moved=1 << 20):
        in_specs = in_specs or [vmem] * len(ins)
        out_specs = out_specs or [vmem] * len(outs)
        return pl.pallas_call(
            kernel,
            grid=grid,
            out_shape=[jax.ShapeDtypeStruct(shape, dtype) for shape, dtype in outs],
            in_specs=in_specs,
            out_specs=out_specs,
            scratch_shapes=list(scratch),
            compiler_params=pltpu.CompilerParams(vmem_limit_bytes=VMEM_LIMIT),
            cost_estimate=pl.CostEstimate(flops=flops, bytes_accessed=moved, transcendentals=0),
            name=name,
        )(*ins)

    def pack_kernel(c_ref, b_ref, out_ref, c_buffer, b_buffer, sems):
        copies = [
            pltpu.make_async_copy(c_ref, c_buffer, sems.at[0]),
            pltpu.make_async_copy(b_ref, b_buffer, sems.at[1]),
        ]
        for copy in copies:
            copy.start()
        for copy in copies:
            copy.wait()
        out_ref[:c_rows, :] = c_buffer[0]
        out_ref[c_rows:, :] = b_buffer[0]

    hbm = pl.BlockSpec(memory_space=pltpu.HBM)
    (given,) = call(
        pack_kernel,
        "pack",
        [pltpu.with_memory_space_constraint(factor, pltpu.HBM) for factor in (factor_c, factor_b)],
        [((c_rows + b_rows, rank), F32)],
        in_specs=[hbm, hbm],
        scratch=[pltpu.VMEM(factor_c.shape, F32), pltpu.VMEM(factor_b.shape, F32), pltpu.SemaphoreType.DMA((2,))],
    )
    others = [swap(given, "ia", q) for q in range(1, n_ia)]

    def load_kernel(t_ref, high_ref, low_ref, buffer_ref, sems):
        copies = [
            pltpu.make_async_copy(
                t_ref.at[pl.ds(s * i_step, i_step)], buffer_ref.at[pl.ds(s * i_step, i_step)], sems.at[s]
            )
            for s in range(steps)
        ]
        for copy in copies:
            copy.start()
        for s, copy in enumerate(copies):
            copy.wait()
            high, low = split(buffer_ref[s * i_step : (s + 1) * i_step].reshape(depth, k_dev))
            high_ref[s * depth : (s + 1) * depth, :] = high
            low_ref[s * depth : (s + 1) * depth, :] = low

    t_parts = call(
        load_kernel,
        "load",
        [pltpu.with_memory_space_constraint(tensor, pltpu.HBM)],
        [((i_dev * j_dev, k_dev), BF16)] * 2,
        in_specs=[hbm],
        scratch=[pltpu.VMEM((i_dev, j_dev, k_dev), F32), pltpu.SemaphoreType.DMA((steps,))],
        moved=8 * size,
    )
    *others, t_high, t_low = lax.optimization_barrier((*others, *t_parts))
    both = jnp.stack([given, *others])
    c_blocks = grow(both[:, :c_rows].reshape(n_ia * c_rows, rank), ja_bits)
    b_blocks = grow(both[:, c_rows:].reshape(n_ia * b_rows, rank), ka_bits)

    def given_kernel(place_ref, c_ref, b_ref, gram_ref, tall_ref, b_out, whole_c, whole_b):
        left, right = c_ref[:, :h], c_ref[:, h:]
        gram_ref[:h, :] = mul3(left, left, TN)
        gram_ref[h : 2 * h, :] = mul3(left, right, TN)
        gram_ref[2 * h :, :] = mul3(right, right, TN)
        ia, ja, ka = place_ref[0], place_ref[1], place_ref[2]
        for p in range(n_c):
            masks = origin(p, ia_bits[::-1] + ja_bits)
            whole_c[(ia ^ masks["ia"]) * n_ja + (ja ^ masks["ja"])] = c_ref[p * c_rows : (p + 1) * c_rows, :]
        for p in range(n_b):
            masks = origin(p, ia_bits[::-1] + ka_bits)
            whole_b[(ia ^ masks["ia"]) * n_ka + (ka ^ masks["ka"])] = b_ref[p * b_rows : (p + 1) * b_rows, :]
        b_out[...] = whole_b[...].reshape(j_dev, rank)
        high, low = split(whole_c[...].reshape(k_dev, rank))
        tall_ref[:k_dev, :] = high
        tall_ref[k_dev : 2 * k_dev, :] = high
        tall_ref[2 * k_dev :, :] = low

    gram_c_part, tall, b_slice = call(
        given_kernel,
        "given",
        [place, c_blocks, b_blocks],
        [((3 * h, h), F32), ((3 * k_dev, rank), BF16), ((j_dev, rank), F32)],
        in_specs=[smem, vmem, vmem],
        scratch=[pltpu.VMEM((n_c, c_rows, rank), F32), pltpu.VMEM((n_b, b_rows, rank), F32)],
        flops=2 * 6 * k_dev * rank * rank,
    )
    gram_c = gram_c_part
    for axis, distance in ka_bits:
        gram_c = gram_c + swap(gram_c, axis, distance)
    all_b = grow(b_blocks, ja_bits[::-1])

    def first_kernel(high_ref, low_ref, tall_ref, b_ref, y_ref, out_ref):
        def step(s, _):
            high, low = high_ref[span(s, depth), :], low_ref[span(s, depth), :]
            wide = jnp.concatenate([high, low, high], axis=1)
            inner = lax.dot_general(wide, tall_ref[...], NN, preferred_element_type=F32).reshape(i_step, j_dev, rank)
            y_ref[span(s, i_step)] = inner
            out_ref[span(s, i_step), :] = jnp.sum(inner * b_ref[...].reshape(1, j_dev, rank), axis=1)
            return 0

        lax.fori_loop(0, steps, step, 0, unroll=2)

    y, parts_a = call(
        first_kernel,
        "first",
        [t_high, t_low, tall, b_slice],
        [((i_dev, j_dev, rank), F32), ((i_dev, rank), F32)],
        flops=6 * size * rank,
        moved=8 * size,
    )

    def invert_a_first_kernel(packed_ref, b_ref, half_ref, cross_ref, gram_ref, m_ref):
        gram_ref[:h, :h] = packed_ref[:h, :]
        gram_ref[:h, h:] = packed_ref[h : 2 * h, :]
        gram_ref[h:, :h] = packed_ref[h : 2 * h, :].T
        gram_ref[h:, h:] = packed_ref[2 * h :, :]
        b = b_ref[...]
        m_ref[...] = gram_ref[...] * mul3(b, b, TN)
        invert_first(m_ref, half_ref, cross_ref)

    halves, cross, gram_c = call(
        invert_a_first_kernel,
        "invert_a_first",
        [gram_c, all_b],
        [((2, h, h), F32), ((h, h), F32), ((rank, rank), F32)],
        scratch=[pltpu.VMEM((rank, rank), F32)],
        flops=5 * 1000 * 1000 * 1000,
    )

    def invert_last_kernel(half_in, cross_ref, out_ref, half_ref):
        half_ref[...] = half_in[...]
        invert_last(half_ref, cross_ref, out_ref)

    stages = [pair for pair in ja_bits if pair[1] > 1] + ka_bits + [pair for pair in ja_bits if pair[1] == 1]
    for at, (axis, distance) in enumerate(stages[:-1]):
        other_a = swap(parts_a, axis, distance)
        if at == 0:
            halves, cross, other_a = lax.optimization_barrier((halves, cross, other_a))
            (inverse_a,) = call(
                invert_last_kernel,
                "invert_a_last",
                [halves, cross],
                [((rank, rank), F32)],
                scratch=[pltpu.VMEM((2, h, h), F32)],
                flops=5 * 1000 * 1000 * 1000,
            )
        if at == 1:
            inverse_a, other_a = lax.optimization_barrier((inverse_a, other_a))
        parts_a = parts_a + other_a
    other_a = swap(parts_a, *stages[-1])

    def solve_a_kernel(place_ref, one_ref, other_ref, inverse_ref, a_ref, own_ref, gram_ref, rows_ref, packed_ref):
        a = mul3(one_ref[...] + other_ref[...], inverse_ref[...])
        a_ref[...] = a
        rows_ref[...] = a.reshape(n_a, a_rows, rank)
        own_ref[...] = rows_ref[place_ref[1] * n_ka + place_ref[2]]
        left, right = a[:, :h], a[:, h:]
        middle = mul3(left, right, TN)
        packed_ref[0, :h, :] = mul3(left, left, TN)
        packed_ref[0, h:, :] = middle[: h // 2]
        packed_ref[1, :h, :] = mul3(right, right, TN)
        packed_ref[1, h:, :] = middle[h // 2 :]
        gram_ref[...] = packed_ref[place_ref[1] & 1]

    a_slice, new_a, gram_a = call(
        solve_a_kernel,
        "solve_a",
        [place, parts_a, other_a, inverse_a],
        [((i_dev, rank), F32), ((a_rows, rank), F32), ((packed, h), F32)],
        in_specs=[smem, vmem, vmem, vmem],
        scratch=[pltpu.VMEM((n_a, a_rows, rank), F32), pltpu.VMEM((2, packed, h), F32)],
    )
    far_gram = swap(gram_a, *ia_bits[0])

    def second_kernel(y_ref, a_ref, out_ref):
        def step(s, total):
            return total + jnp.sum(y_ref[span(s, i_step)] * a_ref[span(s, i_step), :][:, None, :], axis=0)

        out_ref[...] = lax.fori_loop(0, steps, step, jnp.zeros((j_dev, rank), F32))

    (parts_b,) = call(
        second_kernel,
        "second",
        [y, a_slice],
        [((j_dev, rank), F32)],
        flops=2 * i_dev * j_dev * rank,
        moved=4 * i_dev * j_dev * rank,
    )
    t_high, t_low, parts_b = lax.optimization_barrier((t_high, t_low, parts_b))

    def turn_kernel(high_ref, low_ref, out_ref):
        def step(s, _):
            out_ref[:k_dev, span(s, depth)] = high_ref[span(s, depth), :].T
            out_ref[k_dev:, span(s, depth)] = low_ref[span(s, depth), :].T
            return 0

        lax.fori_loop(0, steps, step, 0)

    (turned,) = call(
        turn_kernel, "turn", [t_high, t_low], [((2 * k_dev, i_dev * j_dev), BF16)], moved=8 * size
    )
    stages_b = ka_bits + ia_bits
    other_b = swap(parts_b, *stages_b[0])
    far_gram, turned, other_b = lax.optimization_barrier((far_gram, turned, other_b))
    gram_a = gram_a + far_gram
    parts_b = parts_b + other_b
    for axis, distance in ia_bits[1:]:
        near_gram = swap(gram_a, axis, distance)
        gram_a = gram_a + near_gram
    gram_a_other = swap(gram_a, "ja", 1)

    def invert_b_first_kernel(place_ref, one_ref, other_ref, gram_c_ref, gram_ref, half_ref, cross_ref, packed_ref, m_ref):
        core = place_ref[1] & 1
        packed_ref[core] = one_ref[...]
        packed_ref[core ^ 1] = other_ref[...]
        gram_ref[:h, :h] = packed_ref[0, :h, :]
        gram_ref[h:, h:] = packed_ref[1, :h, :]
        gram_ref[: h // 2, h:] = packed_ref[0, h:, :]
        gram_ref[h // 2 : h, h:] = packed_ref[1, h:, :]
        gram_ref[h:, :h] = gram_ref[:h, h:].T
        m_ref[...] = gram_ref[...] * gram_c_ref[...]
        invert_first(m_ref, half_ref, cross_ref)

    gram_a, halves, cross = call(
        invert_b_first_kernel,
        "invert_b_first",
        [place, gram_a, gram_a_other, gram_c],
        [((rank, rank), F32), ((2, h, h), F32), ((h, h), F32)],
        in_specs=[smem, vmem, vmem, vmem],
        scratch=[pltpu.VMEM((2, packed, h), F32), pltpu.VMEM((rank, rank), F32)],
        flops=5 * 1000 * 1000 * 1000,
    )

    for at, (axis, distance) in enumerate(stages_b[1:-1], 1):
        other_b = swap(parts_b, axis, distance)
        if at == len(stages_b) - 2:
            halves, cross, other_b = lax.optimization_barrier((halves, cross, other_b))
        parts_b = parts_b + other_b
    other_b = swap(parts_b, *stages_b[-1])
    (inverse_b,) = call(
        invert_last_kernel,
        "invert_b_last",
        [halves, cross],
        [((rank, rank), F32)],
        scratch=[pltpu.VMEM((2, h, h), F32)],
        flops=5 * 1000 * 1000 * 1000,
    )

    def solve_b_kernel(place_ref, one_ref, other_ref, inverse_ref, b_ref, own_ref, rows_ref):
        b = mul3(one_ref[...] + other_ref[...], inverse_ref[...])
        b_ref[...] = b
        rows_ref[...] = b.reshape(n_b, b_rows, rank)
        own_ref[...] = rows_ref[place_ref[0] * n_ka + place_ref[2]]

    b_new_slice, new_b = call(
        solve_b_kernel,
        "solve_b",
        [place, parts_b, other_b, inverse_b],
        [((j_dev, rank), F32), ((b_rows, rank), F32)],
        in_specs=[smem, vmem, vmem, vmem],
        scratch=[pltpu.VMEM((n_b, b_rows, rank), F32)],
    )

    first_b = swap(b_new_slice, *ja_bits[0])

    def third_kernel(turned_ref, a_ref, b_ref, out_ref):
        def step(s, total):
            high, low = split((a_ref[span(s, i_step), :][:, None, :] * b_ref[...][None]).reshape(depth, rank))
            both = lax.dot_general(turned_ref[:, span(s, depth)], high, NN, preferred_element_type=F32)
            more = lax.dot_general(turned_ref[:k_dev, span(s, depth)], low, NN, preferred_element_type=F32)
            return total + (both[:k_dev] + (both[k_dev:] + more))

        out_ref[...] = lax.fori_loop(0, steps, step, jnp.zeros((k_dev, rank), F32), unroll=2)

    (parts_c,) = call(
        third_kernel,
        "third",
        [turned, a_slice, b_new_slice],
        [((k_dev, rank), F32)],
        flops=6 * size * rank,
        moved=4 * size,
    )
    first_b, parts_c = lax.optimization_barrier((first_b, parts_c))
    all_b_new = grow(jnp.concatenate([b_new_slice, first_b], axis=0), ja_bits[1:])
    sums_c = lax.all_to_all(parts_c.reshape(n_c, c_rows, rank), ("ia", "ja"), split_axis=0, concat_axis=0)

    def invert_c_kernel(b_ref, gram_a_ref, inverse_ref, m_ref, half_ref, cross_ref):
        b = b_ref[...]
        m_ref[...] = gram_a_ref[...] * mul3(b, b, TN)
        invert_first(m_ref, half_ref, cross_ref)
        invert_last(half_ref, cross_ref, inverse_ref)

    (inverse_c,) = call(
        invert_c_kernel,
        "invert_c",
        [all_b_new, gram_a],
        [((rank, rank), F32)],
        scratch=invert_scratch(rank),
        flops=10 * 1000 * 1000 * 1000,
    )

    def solve_c_kernel(sums_ref, inverse_ref, out_ref):
        out_ref[...] = mul3(tree(sums_ref[q] for q in range(n_c)), inverse_ref[...])

    (new_c,) = call(solve_c_kernel, "solve_c", [sums_c, inverse_c], [((c_rows, rank), F32)])
    return (new_a[None], new_b[None], new_c[None])


def solution(mesh):
    sizes = [mesh.shape[axis] for axis in ("ia", "ja", "ka")]
    return jax.shard_map(
        functools.partial(on_device, *sizes),
        mesh=mesh,
        in_specs=(P("ia", "ja", "ka"), P("ja", ("ia", "ka"), None), P("ka", ("ia", "ja"), None)),
        out_specs=(
            P("ia", ("ja", "ka"), None),
            P("ja", ("ia", "ka"), None),
            P("ka", ("ia", "ja"), None),
        ),
        check_vma=False,
    )
```
